512 devices in a mesh: ctx: 64 (over y_hi, z, core), tsp: 8 (over x, y_lo).
Axes of the slice: x: 4, y: 8 (y_hi: 4, y_lo: 2; y = y_hi * 2 + y_lo), z: 8, core: 2. Of those that a mesh axis runs over, the one named last changes fastest.
Arguments:
- queries: bfloat16 [2, 8192, 4096], P(None, 'ctx', 'tsp'), may hold values from -5 to 5
- kv_cache: bfloat16 [2, 8192, 1024], P(None, ('ctx', 'tsp')), may hold values from -5 to 5
- grad_out: bfloat16 [2, 8192, 4096], P(None, 'ctx', 'tsp'), may hold values from -6 to 6
- positions: int32 [8192], P('ctx'), may hold values from 0 to 4095, as said below
Outputs:
- attn_out: bfloat16 [2, 8192, 4096], P(None, 'ctx', 'tsp')
- grad_queries: bfloat16 [2, 8192, 4096], P(None, 'ctx', 'tsp')
- grad_cache: bfloat16 [2, 8192, 1024], P(None, ('ctx', 'tsp'))
The draws below stay inside these ranges and needn't reach their ends.
Inputs may be any that keep to these rules, and one draw needn't show every extreme that they name: positions[0] = 0, and every later entry is 0 where a document begins or the entry before it plus 1; the sequence holds two to 4 documents.
All inputs are finite; a program needn't handle non-finite values.
Results may differ from the reference program's by a relative error of at most 0.022.
Values may be sent and summed in bfloat16 or wider, within the bound.
A program may use at most 64 MiB of HBM per device.

```python
import jax
import jax.numpy as jnp
from jax import lax

QUERY_HEADS = 32
KEY_VALUE_HEADS = 8
HEAD_DIMENSION = 128
SHARING_LAYERS = 2
DOCS = 4
CONTEXT_ROWS = 128
WINDOW = 1024
SEQUENCE_TOKENS = 8192


def token_positions(key):
    half = SEQUENCE_TOKENS // 2
    later = jax.random.randint(jax.random.fold_in(key, 101), (DOCS - 2,), half + 1, SEQUENCE_TOKENS)
    starts = jnp.concatenate([jnp.zeros((1,), jnp.int32), jnp.full((1,), half, jnp.int32), later.astype(jnp.int32)])
    index = jnp.arange(SEQUENCE_TOKENS, dtype=jnp.int32)
    begun = jnp.where(starts[None, :] <= index[:, None], starts[None, :], 0)
    return index - jnp.max(begun, axis=1)


def draw_positions(key, part):
    return token_positions(key)


def draw_queries(key, part):
    key = jax.random.fold_in(key, 5)
    return jnp.clip(jax.random.normal(key, (SHARING_LAYERS, SEQUENCE_TOKENS, QUERY_HEADS * HEAD_DIMENSION), jnp.float32), -5.0, 5.0).astype(jnp.bfloat16)


def draw_kv_cache(key, part):
    key = jax.random.fold_in(key, 3)
    return jnp.clip(jax.random.normal(key, (2, SEQUENCE_TOKENS, KEY_VALUE_HEADS * HEAD_DIMENSION), jnp.float32), -5.0, 5.0).astype(jnp.bfloat16)


def block_scale(key, extent, shards, low, top_value):
    def one(axis_at, parts):
        heights = jax.random.uniform(jax.random.fold_in(jax.random.fold_in(key, 6), axis_at), (parts,), jnp.float32, low / len(shards), top_value / len(shards))
        return jnp.repeat(jnp.exp(heights), extent[axis_at] // parts).reshape((-1,) + (1,) * (len(extent) - axis_at - 1))

    loudness = one(*shards[0])
    for cut in shards[1:]:
        loudness = loudness * one(*cut)
    return loudness


def noise(stream_key, shape, scale, most, pieces=(), kind=jnp.bfloat16):
    values = jax.random.normal(stream_key, shape, jnp.float32) * scale
    if len(pieces) > 0:
        values = block_scale(stream_key, shape, pieces, -0.22, 0.18) * values
    return jnp.clip(values, min=-most, max=most).astype(kind)


def setup_inputs(seed: int = 0) -> dict:
    splits = jax.random.split(jax.random.key(seed), 5)
    return {
        "queries": draw_queries(jax.random.fold_in(splits[4], 71), 0),
        "kv_cache": draw_kv_cache(jax.random.fold_in(splits[4], 71), 0),
        "grad_out": noise(splits[2], (SHARING_LAYERS, SEQUENCE_TOKENS, QUERY_HEADS * HEAD_DIMENSION), 1.0, 6.0, ((1, 64), (2, 8))),
        "positions": draw_positions(jax.random.fold_in(splits[4], 71), 0),
    }


def reference(queries, kv_cache, grad_out, positions):
    group_length = QUERY_HEADS // KEY_VALUE_HEADS
    scaling = HEAD_DIMENSION ** -0.5
    key_value_width = KEY_VALUE_HEADS * HEAD_DIMENSION
    cache_section = WINDOW + CONTEXT_ROWS
    padding = jnp.zeros((WINDOW, key_value_width), jnp.float32)
    key_padded = jnp.concatenate([padding, kv_cache[0].astype(jnp.float32)], axis=0)
    value_padded = jnp.concatenate([padding, kv_cache[1].astype(jnp.float32)], axis=0)
    row_index = jnp.arange(CONTEXT_ROWS, dtype=jnp.int32)
    col_index = jnp.arange(cache_section, dtype=jnp.int32)
    distance = row_index[:, None] + WINDOW - col_index[None, :]

    def one_block(grads, block):
        start_position = (block * CONTEXT_ROWS).astype(jnp.int32)
        query_rows = lax.dynamic_slice_in_dim(queries, start_position, CONTEXT_ROWS, 1).astype(jnp.float32)
        query_rows = query_rows.reshape(SHARING_LAYERS, CONTEXT_ROWS, KEY_VALUE_HEADS, group_length, HEAD_DIMENSION)
        upstream_gradient = lax.dynamic_slice_in_dim(grad_out, start_position, CONTEXT_ROWS, 1).astype(jnp.float32)
        upstream_gradient = upstream_gradient.reshape(SHARING_LAYERS, CONTEXT_ROWS, KEY_VALUE_HEADS, group_length, HEAD_DIMENSION)
        current_pos = lax.dynamic_slice_in_dim(positions, start_position, CONTEXT_ROWS, 0)
        key_row_block = lax.dynamic_slice_in_dim(key_padded, start_position, cache_section, 0).reshape(cache_section, KEY_VALUE_HEADS, HEAD_DIMENSION)
        value_row_block = lax.dynamic_slice_in_dim(value_padded, start_position, cache_section, 0).reshape(cache_section, KEY_VALUE_HEADS, HEAD_DIMENSION)
        visible = (distance >= 0) & (distance <= current_pos[:, None]) & (distance < WINDOW)
        scores = jnp.einsum("lrkgd,ckd->lkgrc", query_rows, key_row_block) * scaling
        scores = jnp.where(visible, scores, -jnp.inf)
        maxima = jnp.max(scores, axis=-1, keepdims=True)
        expo = jnp.exp(scores - maxima)
        probs = expo / jnp.sum(expo, axis=-1, keepdims=True)
        probs_low = lax.optimization_barrier(probs.astype(jnp.bfloat16)).astype(jnp.float32)
        attended = jnp.einsum("lkgrc,ckd->lrkgd", probs_low, value_row_block)
        attended_low = lax.optimization_barrier(attended.astype(jnp.bfloat16))
        delta = jnp.sum(upstream_gradient * attended_low.astype(jnp.float32), axis=-1)
        delta = jnp.transpose(delta, (0, 2, 3, 1))[..., None]
        dprobs = jnp.einsum("lrkgd,ckd->lkgrc", upstream_gradient, value_row_block)
        dscores = lax.optimization_barrier((probs * (dprobs - delta)).astype(jnp.bfloat16)).astype(jnp.float32)
        grad_q = scaling * jnp.einsum("lkgrc,ckd->lrkgd", dscores, key_row_block)
        grad_k = scaling * jnp.einsum("lkgrc,lrkgd->ckd", dscores, query_rows)
        grad_v = jnp.einsum("lkgrc,lrkgd->ckd", probs_low, upstream_gradient)
        update = jnp.stack([grad_k.reshape(cache_section, key_value_width), grad_v.reshape(cache_section, key_value_width)])
        current = lax.dynamic_slice_in_dim(grads, start_position, cache_section, 1)
        grads = lax.dynamic_update_slice_in_dim(grads, current + update, start_position, 1)
        out_block = attended_low.reshape(SHARING_LAYERS, CONTEXT_ROWS, QUERY_HEADS * HEAD_DIMENSION)
        grad_block = grad_q.astype(jnp.bfloat16).reshape(SHARING_LAYERS, CONTEXT_ROWS, QUERY_HEADS * HEAD_DIMENSION)
        return grads, (out_block, grad_block)

    initial = jnp.zeros((2, WINDOW + SEQUENCE_TOKENS, key_value_width), jnp.float32)
    block_ids = jnp.arange(SEQUENCE_TOKENS // CONTEXT_ROWS, dtype=jnp.int32)
    grads, (out_blocks, grad_blocks) = lax.scan(one_block, initial, block_ids)
    attn_out = jnp.transpose(out_blocks, (1, 0, 2, 3)).reshape(SHARING_LAYERS, SEQUENCE_TOKENS, QUERY_HEADS * HEAD_DIMENSION)
    grad_queries = jnp.transpose(grad_blocks, (1, 0, 2, 3)).reshape(SHARING_LAYERS, SEQUENCE_TOKENS, QUERY_HEADS * HEAD_DIMENSION)
    grad_cache = grads[:, WINDOW:, :].astype(jnp.bfloat16)
    return attn_out, grad_queries, grad_cache
```

```python
import functools
import math

import jax
import jax.numpy as jnp
from jax import lax
from jax.experimental import pallas as pl
from jax.experimental.pallas import tpu as pltpu
from jax.sharding import PartitionSpec as P

LAYERS = 2
GROUP = 4
DIM = 128
ROWS = 128
SPAN = 8
NEAR = SPAN // 2
SLOTS = SPAN + 1
HEADS = LAYERS * GROUP
COLS = HEADS * ROWS
CHUNK = 256
SCALE = DIM ** (-0.5)
TO_EXP2 = SCALE * math.log2(math.e)
LOW = -1e30
MESH = pl.DeviceIdType.MESH
F32 = jnp.float32
BF16 = jnp.bfloat16


def dot(a, b):
    return lax.dot_general(a, b, (((1,), (0,)), ((), ())), preferred_element_type=F32)


def kernel(
    blocks, lanes,
    q_hbm, kv_hbm, g_hbm, pos_ref,
    o_hbm, dq_hbm, dkv_ref,
    kv, qs, gs, q_t, g_t, keys, vals, k_t, v_t, bias,
    top, total, tops, expo, probs, dprobs, dscores, delta, o_acc,
    pair_out, pair_in, ready, landed, o_out, dq_out,
    in_sem, out_sem, kv_send, kv_recv, pair_send, pair_recv,
    back_send, back_recv, swap_send, swap_recv,
):
    c = lax.axis_index("ctx")
    t = lax.axis_index("tsp")
    core = lax.rem(c, 2)
    partner = (c + 1 - 2 * core, t)
    piece = ROWS // lanes

    def lane(i):
        return lax.rem(t + i, lanes)

    def ahead(d):
        return lax.rem(c + 2 * d, blocks)

    def behind(d):
        return lax.rem(c + blocks - 2 * d, blocks)

    barrier = pltpu.get_barrier_semaphore()
    pl.semaphore_signal(barrier, inc=1, device_id=partner, device_id_type=MESH)
    for d in range(NEAR + 1):
        def hello(i, _, d=d):
            pl.semaphore_signal(barrier, inc=1, device_id=(behind(d), lane(i)), device_id_type=MESH)
            return 0
        lax.fori_loop(1 if d == 0 else 0, lanes, hello, 0)

    kv_copy = pltpu.make_async_copy(kv_hbm, kv, in_sem.at[0])
    kv_copy.start()
    def loads():
        out = []
        for l in range(LAYERS):
            for g in range(GROUP):
                n = l * GROUP + g
                cut = pl.ds(g * DIM, DIM)
                out.append(pltpu.make_async_copy(q_hbm.at[l, :, cut], qs.at[pl.ds(n * ROWS, ROWS)], in_sem.at[1 + n]))
                out.append(pltpu.make_async_copy(g_hbm.at[l, :, cut], gs.at[pl.ds(n * ROWS, ROWS)], in_sem.at[1 + HEADS + n]))
        return out
    for copy in loads():
        copy.start()
    kv_copy.wait()
    pl.semaphore_wait(barrier, (NEAR + 1) * lanes)

    def kv_piece(kind, d, i):
        to = lane(i)
        place = (keys if kind == 0 else vals)
        return pltpu.make_async_remote_copy(
            kv.at[kind, :, pl.ds(pl.multiple_of(to * DIM, DIM), DIM)],
            place.at[2 * d, pl.ds(pl.multiple_of(t * piece, piece), piece)],
            kv_send.at[kind, d],
            kv_recv.at[kind, d],
            device_id=(ahead(d), to),
            device_id_type=MESH,
        )
    def own_piece(kind):
        place = (keys if kind == 0 else vals)
        return pltpu.make_async_copy(
            kv.at[kind, :, pl.ds(pl.multiple_of(t * DIM, DIM), DIM)],
            place.at[0, pl.ds(pl.multiple_of(t * piece, piece), piece)],
            in_sem.at[1 + 2 * HEADS + kind],
        )
    for kind in range(2):
        own_piece(kind).start()
        for d in range(NEAR + 1):
            def send(i, _, kind=kind, d=d):
                kv_piece(kind, d, i).start()
                return 0
            lax.fori_loop(1 if d == 0 else 0, lanes, send, 0)

    def whole(buf, kind, d, rows=ROWS):
        return pltpu.make_async_remote_copy(
            buf.at[0, pl.ds(0, rows)], buf.at[0, pl.ds(0, rows)],
            kv_send.at[kind, d], kv_recv.at[kind, d],
            device_id=partner, device_id_type=MESH,
        )
    def relay(kind, d):
        place = (keys if kind == 0 else vals)
        e = d - core
        return pltpu.make_async_remote_copy(
            place.at[2 * d], place.at[2 * e + 1],
            pair_send.at[kind, e], pair_recv.at[kind, e],
            device_id=partner, device_id_type=MESH,
        )
    def relayed(kind, e):
        place = (keys if kind == 0 else vals)
        return pltpu.make_async_remote_copy(
            place.at[2 * (e + core)], place.at[2 * e + 1],
            pair_send.at[kind, e], pair_recv.at[kind, e],
            device_id=partner, device_id_type=MESH,
        )

    for copy in loads():
        copy.wait()
    for n in range(HEADS):
        part = pl.ds(n * ROWS, ROWS)
        q_t[:, part] = qs[part].T
        g_t[:, part] = gs[part].T
    pos = pos_ref[...]
    base = lax.broadcasted_iota(jnp.int32, (ROWS, ROWS), 1) - lax.broadcasted_iota(jnp.int32, (ROWS, ROWS), 0)
    def mask(o, _):
        distance = base + o * ROWS
        visible = (distance >= 0) & (distance <= pos) & (distance < SPAN * ROWS)
        bias[o] = jnp.where(visible, 0.0, -jnp.inf)
        return 0
    lax.fori_loop(0, SLOTS, mask, 0)
    top[...] = jnp.full(top.shape, LOW, F32)
    total[...] = jnp.zeros(total.shape, F32)

    def chunks():
        return [pl.ds(i * CHUNK, CHUNK) for i in range(COLS // CHUNK)]

    def rows_of(o):
        if isinstance(o, int):
            return pl.ds(o * ROWS, ROWS)
        return pl.ds(pl.multiple_of(o * ROWS, ROWS), ROWS)

    def score(o):
        block = keys[o]
        hide = jnp.concatenate([bias[o]] * (CHUNK // ROWS), axis=1)
        for cut in chunks():
            s = dot(block, q_t[:, cut]) + hide
            before = top[:, cut]
            now = jnp.maximum(before, jnp.max(s, axis=0, keepdims=True))
            e = jnp.exp2((s - now) * TO_EXP2)
            total[:, cut] = total[:, cut] * jnp.exp2((before - now) * TO_EXP2) + jnp.sum(e, axis=0, keepdims=True)
            top[:, cut] = now
            tops[o, :, cut] = now
            expo[rows_of(o), cut] = e
        k_t[:, rows_of(o)] = block.T

    def value(o):
        block = vals[o]
        for cut in chunks():
            dprobs[rows_of(o), cut] = dot(block, g_t[:, cut])
        v_t[:, rows_of(o)] = block.T

    def gather(kind, use):
        own_piece(kind).wait()
        whole((keys if kind == 0 else vals), kind, 0, ROWS - piece).wait_recv()
        @pl.when(core == 0)
        def _():
            relay(kind, 0).start()
        use(0)
        def step(d, _):
            whole((keys if kind == 0 else vals), kind, d).wait_recv()
            @pl.when(d - core < NEAR)
            def _():
                relay(kind, d).start()
            use(2 * d)
            relayed(kind, d - 1).wait_recv()
            use(2 * d - 1)
            return 0
        lax.fori_loop(1, NEAR + 1, step, 0)

    gather(0, score)

    def factor(o, cut):
        return tops[o, :, cut]

    inverse = 1.0 / total[...]
    last = top[...]
    def scales(o, _):
        tops[o] = jnp.exp2((tops[o] - last) * TO_EXP2) * inverse
        return 0
    lax.fori_loop(0, SLOTS, scales, 0)
    def soft(o, _):
        for cut in chunks():
            probs[rows_of(o), cut] = (expo[rows_of(o), cut] * factor(o, cut)).astype(BF16)
        return 0
    lax.fori_loop(0, SLOTS, soft, 0)

    def swap(kind, e):
        return pltpu.make_async_remote_copy(
            pair_out.at[kind, e], pair_in.at[kind, e],
            swap_send.at[kind, e], swap_recv.at[kind, e],
            device_id=partner, device_id_type=MESH,
        )
    def back_piece(kind, d, i):
        to = lane(i)
        return pltpu.make_async_remote_copy(
            ready.at[kind, d, pl.ds(pl.multiple_of(to * piece, piece), piece)],
            landed.at[kind, d, t],
            back_send.at[kind, d],
            back_recv.at[kind, d],
            device_id=(behind(d), to),
            device_id_type=MESH,
        )
    def give_back(kind, left, right):
        def odd(i, _):
            e = NEAR - 1 - i
            pair_out[kind, e] = dot(left[rows_of(2 * e + 1), :], right[...])
            swap(kind, e).start()
            return 0
        lax.fori_loop(0, NEAR, odd, 0)
        def even(i, _):
            d = NEAR - i
            mine = dot(left[rows_of(2 * d), :], right[...])
            e = d - core
            paired = (e >= 0) & (e < NEAR)
            @pl.when(paired)
            def _():
                swap(kind, e).wait_recv()
                both = mine + pair_in[kind, e]
                ready[kind, d] = (both if kind == 1 else both * SCALE).astype(BF16)
            @pl.when(jnp.logical_not(paired))
            def _():
                ready[kind, d] = (mine if kind == 1 else mine * SCALE).astype(BF16)
            def send(i, _):
                back_piece(kind, d, i).start()
                return 0
            lax.fori_loop(jnp.where(d == 0, 1, 0), lanes, send, 0)
            return 0
        lax.fori_loop(0, NEAR + 1, even, 0)
        landed[kind, 0, t] = ready[kind, 0, pl.ds(pl.multiple_of(t * piece, piece), piece), :]

    give_back(1, probs, gs)

    gather(1, value)

    for i, cut in enumerate(chunks()):
        o = dot(v_t[...], probs[:, cut]).astype(BF16)
        o_acc[:, cut] = o
        delta[:, cut] = jnp.sum(o.astype(F32) * g_t[:, cut].astype(F32), axis=0, keepdims=True)

    def soft_back(o, _):
        for cut in chunks():
            p = expo[rows_of(o), cut] * factor(o, cut)
            dscores[rows_of(o), cut] = (p * (dprobs[rows_of(o), cut] - delta[:, cut])).astype(BF16)
        return 0
    lax.fori_loop(0, SLOTS, soft_back, 0)

    give_back(0, dscores, qs)

    for n in range(HEADS):
        l, g = n // GROUP, n % GROUP
        part = pl.ds(n * ROWS, ROWS)
        o_out[l, :, pl.ds(g * DIM, DIM)] = o_acc[:, part].T
    o_copy = pltpu.make_async_copy(o_out, o_hbm, out_sem.at[0])
    o_copy.start()
    for i, cut in enumerate(chunks()):
        dq = (dot(k_t[...], dscores[:, cut]) * SCALE).astype(BF16)
        for j in range(CHUNK // ROWS):
            n = i * (CHUNK // ROWS) + j
            l, g = n // GROUP, n % GROUP
            dq_out[l, :, pl.ds(g * DIM, DIM)] = dq[:, j * ROWS:(j + 1) * ROWS].T
    dq_copy = pltpu.make_async_copy(dq_out, dq_hbm, out_sem.at[1])
    dq_copy.start()

    def back_whole(kind, d, count):
        return pltpu.make_async_remote_copy(
            landed.at[0, 0, pl.ds(0, count)], landed.at[0, 0, pl.ds(0, count)],
            back_send.at[kind, d], back_recv.at[kind, d],
            device_id=partner, device_id_type=MESH,
        )
    for kind in (1, 0):
        for d in range(NEAR + 1):
            back_whole(kind, d, lanes - (d == 0)).wait_recv()
        for i in range(lanes):
            acc = landed[kind, 0, i].astype(F32)
            for d in range(1, NEAR + 1):
                acc = acc + landed[kind, d, i].astype(F32)
            dkv_ref[kind, :, pl.ds(i * DIM, DIM)] = acc.astype(BF16)

    for kind in range(2):
        for d in range(NEAR + 1):
            whole(keys, kind, d, ROWS - (piece if d == 0 else 0)).wait_send()
            back_whole(kind, d, lanes - (d == 0)).wait_send()
        for e in range(NEAR):
            relayed(kind, e).wait_send()
            swap(kind, e).wait_send()
    o_copy.wait()
    dq_copy.wait()


def on_device(blocks, lanes, queries, kv_cache, grad_out, positions):
    piece = kv_cache.shape[1]
    wide = kv_cache.shape[2]
    sem = pltpu.SemaphoreType.DMA
    any_spec = pl.BlockSpec(memory_space=pl.ANY)
    vmem_spec = pl.BlockSpec(memory_space=pltpu.VMEM)
    return pl.pallas_call(
        functools.partial(kernel, blocks, lanes),
        out_shape=(
            jax.ShapeDtypeStruct(queries.shape, BF16),
            jax.ShapeDtypeStruct(queries.shape, BF16),
            jax.ShapeDtypeStruct(kv_cache.shape, BF16),
        ),
        in_specs=[any_spec, any_spec, any_spec, vmem_spec],
        out_specs=(any_spec, any_spec, vmem_spec),
        scratch_shapes=[
            pltpu.VMEM((2, piece, wide), BF16),
            pltpu.VMEM((COLS, DIM), BF16),
            pltpu.VMEM((COLS, DIM), BF16),
            pltpu.VMEM((DIM, COLS), BF16),
            pltpu.VMEM((DIM, COLS), BF16),
            pltpu.VMEM((SLOTS, ROWS, DIM), BF16),
            pltpu.VMEM((SLOTS, ROWS, DIM), BF16),
            pltpu.VMEM((DIM, SLOTS * ROWS), BF16),
            pltpu.VMEM((DIM, SLOTS * ROWS), BF16),
            pltpu.VMEM((SLOTS, ROWS, ROWS), F32),
            pltpu.VMEM((1, COLS), F32),
            pltpu.VMEM((1, COLS), F32),
            pltpu.VMEM((SLOTS, 1, COLS), F32),
            pltpu.VMEM((SLOTS * ROWS, COLS), F32),
            pltpu.VMEM((SLOTS * ROWS, COLS), BF16),
            pltpu.VMEM((SLOTS * ROWS, COLS), F32),
            pltpu.VMEM((SLOTS * ROWS, COLS), BF16),
            pltpu.VMEM((1, COLS), F32),
            pltpu.VMEM((DIM, COLS), BF16),
            pltpu.VMEM((2, NEAR, ROWS, DIM), F32),
            pltpu.VMEM((2, NEAR, ROWS, DIM), F32),
            pltpu.VMEM((2, NEAR + 1, ROWS, DIM), BF16),
            pltpu.VMEM((2, NEAR + 1, lanes, piece, DIM), BF16),
            pltpu.VMEM(queries.shape, BF16),
            pltpu.VMEM(queries.shape, BF16),
            sem((3 + 2 * HEADS,)),
            sem((2,)),
            sem((2, NEAR + 1)),
            sem((2, NEAR + 1)),
            sem((2, NEAR)),
            sem((2, NEAR)),
            sem((2, NEAR + 1)),
            sem((2, NEAR + 1)),
            sem((2, NEAR)),
            sem((2, NEAR)),
        ],
        compiler_params=pltpu.CompilerParams(
            collective_id=0, has_side_effects=True, vmem_limit_bytes=48 * 1024 * 1024
        ),
    )(queries, kv_cache, grad_out, positions.reshape(1, ROWS))


def solution(mesh):
    return jax.shard_map(
        functools.partial(on_device, mesh.shape["ctx"], mesh.shape["tsp"]),
        mesh=mesh,
        in_specs=(
            P(None, "ctx", "tsp"),
            P(None, ("ctx", "tsp"), None),
            P(None, "ctx", "tsp"),
            P("ctx"),
        ),
        out_specs=(P(None, "ctx", "tsp"), P(None, "ctx", "tsp"), P(None, ("ctx", "tsp"), None)),
        check_vma=False,
    )
```

```python
import functools
import math

import jax
import jax.numpy as jnp
from jax import lax
from jax.experimental import pallas as pl
from jax.experimental.pallas import tpu as pltpu
from jax.sharding import PartitionSpec as P

LAYERS = 2
GROUP = 4
DIM = 128
ROWS = 128
SPAN = 8
NEAR = SPAN // 2
SLOTS = SPAN + 1
HEADS = LAYERS * GROUP
DIRECT = (2, 4, 1, 0)
COLS = HEADS * ROWS
CHUNK = 256
SCALE = DIM ** (-0.5)
TO_EXP2 = SCALE * math.log2(math.e)
LOW = -1e30
MESH = pl.DeviceIdType.MESH
F32 = jnp.float32
BF16 = jnp.bfloat16


def dot(a, b):
    return lax.dot_general(a, b, (((1,), (0,)), ((), ())), preferred_element_type=F32)


def kernel(
    blocks, lanes,
    q_hbm, kv_hbm, g_hbm, pos_hbm,
    o_out, dq_out, dkv_ref,
    kv, pos_ref, qs, gs, q_t, g_t, keys, vals, k_t, v_t, bias,
    top, total, tops, expo, probs, dprobs, dscores, delta, o_acc,
    mine, pair_out, pair_in, ready, landed,
    in_sem, kv_send, kv_recv, pair_send, pair_recv,
    back_send, back_recv, swap_send, swap_recv,
):
    c = lax.axis_index("ctx")
    t = lax.axis_index("tsp")
    core = lax.rem(c, 2)
    partner = (c + 1 - 2 * core, t)
    piece = ROWS // lanes

    def lane(i):
        return lax.rem(t + i, lanes)

    chip = c // 2

    def ahead(d):
        return lax.rem(c + 2 * d, blocks)

    def behind(d):
        return lax.rem(c + blocks - 2 * d, blocks)

    def has_ahead(d):
        return chip + d < blocks // 2

    def has_behind(d):
        return chip >= d

    barrier = pltpu.get_barrier_semaphore()
    pl.semaphore_signal(barrier, inc=1, device_id=partner, device_id_type=MESH)
    for d in DIRECT:
        def hello(i, _, d=d):
            pl.semaphore_signal(barrier, inc=1, device_id=(behind(d), lane(i)), device_id_type=MESH)
            return 0
        @pl.when(has_behind(d))
        def _(d=d, hello=hello):
            lax.fori_loop(1 if d == 0 else 0, lanes, hello, 0)

    kv_copy = pltpu.make_async_copy(kv_hbm, kv, in_sem.at[0])
    kv_copy.start()
    pos_copy = pltpu.make_async_copy(pos_hbm, pos_ref, in_sem.at[3 + 2 * HEADS])
    pos_copy.start()
    def loads():
        out = []
        for l in range(LAYERS):
            for g in range(GROUP):
                n = l * GROUP + g
                cut = pl.ds(g * DIM, DIM)
                out.append(pltpu.make_async_copy(q_hbm.at[l, :, cut], qs.at[pl.ds(n * ROWS, ROWS)], in_sem.at[1 + n]))
                out.append(pltpu.make_async_copy(g_hbm.at[l, :, cut], gs.at[pl.ds(n * ROWS, ROWS)], in_sem.at[1 + HEADS + n]))
        return out
    for copy in loads():
        copy.start()
    kv_copy.wait()
    pl.semaphore_wait(barrier, lanes * (1 + sum(jnp.where(has_ahead(d), 1, 0) for d in DIRECT[:-1])))

    def kv_piece(kind, d, i):
        to = lane(i)
        place = (keys if kind == 0 else vals)
        return pltpu.make_async_remote_copy(
            kv.at[kind, :, pl.ds(pl.multiple_of(to * DIM, DIM), DIM)],
            place.at[d, pl.ds(pl.multiple_of(t * piece, piece), piece)],
            kv_send.at[kind, d],
            kv_recv.at[kind, d],
            device_id=(ahead(d), to),
            device_id_type=MESH,
        )
    def own_piece(kind):
        place = (keys if kind == 0 else vals)
        return pltpu.make_async_copy(
            kv.at[kind, :, pl.ds(pl.multiple_of(t * DIM, DIM), DIM)],
            place.at[0, pl.ds(pl.multiple_of(t * piece, piece), piece)],
            in_sem.at[1 + 2 * HEADS + kind],
        )
    for kind in range(2):
        own_piece(kind).start()
        for d in DIRECT:
            def send(i, _, kind=kind, d=d):
                kv_piece(kind, d, i).start()
                return 0
            @pl.when(has_ahead(d))
            def _(d=d, send=send):
                lax.fori_loop(1 if d == 0 else 0, lanes, send, 0)

    def whole(buf, kind, d, rows=ROWS):
        return pltpu.make_async_remote_copy(
            buf.at[0, pl.ds(0, rows)], buf.at[0, pl.ds(0, rows)],
            kv_send.at[kind, d], kv_recv.at[kind, d],
            device_id=partner, device_id_type=MESH,
        )
    def relay(kind, d):
        place = (keys if kind == 0 else vals)
        e = d - core
        return pltpu.make_async_remote_copy(
            place.at[d], place.at[NEAR + 1 + e],
            pair_send.at[kind, e], pair_recv.at[kind, e],
            device_id=partner, device_id_type=MESH,
        )
    def relayed(kind, e):
        place = (keys if kind == 0 else vals)
        return pltpu.make_async_remote_copy(
            place.at[e + core], place.at[NEAR + 1 + e],
            pair_send.at[kind, e], pair_recv.at[kind, e],
            device_id=partner, device_id_type=MESH,
        )

    for d in range(1, NEAR + 1):
        @pl.when(jnp.logical_not(has_behind(d)))
        def _(d=d):
            keys[d] = jnp.zeros((ROWS, DIM), BF16)
            vals[d] = jnp.zeros((ROWS, DIM), BF16)
        @pl.when(jnp.logical_not(has_ahead(d)))
        def _(d=d):
            for kind in range(2):
                landed[kind, d] = jnp.zeros(landed.shape[2:], BF16)

    for copy in loads():
        copy.wait()
    for n in range(HEADS):
        part = pl.ds(n * ROWS, ROWS)
        q_t[:, part] = qs[part].T
        g_t[:, part] = gs[part].T
    pos_copy.wait()
    pos = pos_ref[...]
    base = lax.broadcasted_iota(jnp.int32, (ROWS, ROWS), 1) - lax.broadcasted_iota(jnp.int32, (ROWS, ROWS), 0)
    def mask(o, _):
        blocks_back = jnp.where(o <= NEAR, 2 * o, 2 * (o - NEAR) - 1)
        distance = base + blocks_back * ROWS
        visible = (distance >= 0) & (distance <= pos) & (distance < SPAN * ROWS)
        bias[o] = jnp.where(visible, 0.0, -jnp.inf)
        return 0
    lax.fori_loop(0, SLOTS, mask, 0)
    top[...] = jnp.full(top.shape, LOW, F32)
    total[...] = jnp.zeros(total.shape, F32)

    def chunks():
        return [pl.ds(i * CHUNK, CHUNK) for i in range(COLS // CHUNK)]

    def rows_of(o):
        if isinstance(o, int):
            return pl.ds(o * ROWS, ROWS)
        return pl.ds(pl.multiple_of(o * ROWS, ROWS), ROWS)

    def score(o):
        block = keys[o]
        hide = jnp.concatenate([bias[o]] * (CHUNK // ROWS), axis=1)
        for cut in chunks():
            s = dot(block, q_t[:, cut]) + hide
            before = top[:, cut]
            now = jnp.maximum(before, jnp.max(s, axis=0, keepdims=True))
            e = jnp.exp2((s - now) * TO_EXP2)
            total[:, cut] = total[:, cut] * jnp.exp2((before - now) * TO_EXP2) + jnp.sum(e, axis=0, keepdims=True)
            top[:, cut] = now
            tops[o, :, cut] = now
            expo[rows_of(o), cut] = e
        k_t[:, rows_of(o)] = block.T

    def value(o):
        block = vals[o]
        for cut in chunks():
            dprobs[rows_of(o), cut] = dot(block, g_t[:, cut])
        v_t[:, rows_of(o)] = block.T

    def forward(kind):
        place = (keys if kind == 0 else vals)
        return pltpu.make_async_remote_copy(
            place.at[2], place.at[3],
            kv_send.at[kind, 3], kv_recv.at[kind, 3],
            device_id=(ahead(1), t), device_id_type=MESH,
        )
    def first(kind):
        @pl.when(has_behind(2))
        def _():
            whole((keys if kind == 0 else vals), kind, 2).wait_recv()
            @pl.when(has_ahead(1))
            def _():
                forward(kind).start()
        relay(kind, 2).start()

    def gather(kind, use, between=None):
        place = (keys if kind == 0 else vals)
        def pair(d):
            e = d - 1 + core
            @pl.when((e >= 0) & (e < NEAR))
            def _():
                relayed(kind, e).wait_recv()
                use(NEAR + 1 + e)
        def order(i):
            return jnp.where(i == 0, 2, jnp.where(i < 3, i - 1, 7 - i))
        use(2)
        def step(i, _):
            d = order(i)
            @pl.when(d == 0)
            def _():
                own_piece(kind).wait()
                whole(place, kind, 0, ROWS - piece).wait_recv()
            @pl.when((d > 0) & has_behind(d))
            def _():
                whole(place, kind, d).wait_recv()
            @pl.when((d - core >= 0) & (d - core < NEAR))
            def _():
                relay(kind, d).start()
            use(d)
            pair(order(i - 1))
            return 0
        lax.fori_loop(1, NEAR + 1, step, 0)
        if between is not None:
            between()
        pair(3)

    first(0)
    gather(0, score, lambda: first(1))

    def factor(o, cut):
        return tops[o, :, cut]

    inverse = 1.0 / total[...]
    last = top[...]
    def scales(o, _):
        tops[o] = jnp.exp2((tops[o] - last) * TO_EXP2) * inverse
        return 0
    lax.fori_loop(0, SLOTS, scales, 0)
    def soft(o, _):
        for cut in chunks():
            probs[rows_of(o), cut] = (expo[rows_of(o), cut] * factor(o, cut)).astype(BF16)
        return 0
    lax.fori_loop(0, SLOTS, soft, 0)

    def swap(kind, e):
        return pltpu.make_async_remote_copy(
            pair_out.at[kind, e], pair_in.at[kind, e],
            swap_send.at[kind, e], swap_recv.at[kind, e],
            device_id=partner, device_id_type=MESH,
        )
    def back_piece(kind, d, i):
        to = lane(i)
        return pltpu.make_async_remote_copy(
            ready.at[kind, d, pl.ds(pl.multiple_of(to * piece, piece), piece)],
            landed.at[kind, d, t],
            back_send.at[kind, d],
            back_recv.at[kind, d],
            device_id=(behind(d), to),
            device_id_type=MESH,
        )
    def give_back(kind, left, right):
        odd = dot(left[pl.ds((NEAR + 1) * ROWS, NEAR * ROWS), :], right[...])
        for e in range(NEAR):
            pair_out[kind, e] = odd[e * ROWS:(e + 1) * ROWS]
            swap(kind, e).start()
        even = dot(left[pl.ds(0, (NEAR + 1) * ROWS), :], right[...])
        for d in range(NEAR + 1):
            mine[kind, d] = even[d * ROWS:(d + 1) * ROWS]
        def step(i, _):
            d = NEAR - i
            e = d - core
            paired = (e >= 0) & (e < NEAR)
            @pl.when(paired)
            def _():
                swap(kind, e).wait_recv()
                both = mine[kind, d] + pair_in[kind, e]
                ready[kind, d] = (both if kind == 1 else both * SCALE).astype(BF16)
            @pl.when(jnp.logical_not(paired))
            def _():
                ready[kind, d] = (mine[kind, d] if kind == 1 else mine[kind, d] * SCALE).astype(BF16)
            def send(i, _):
                back_piece(kind, d, i).start()
                return 0
            lax.fori_loop(jnp.where(d == 0, 1, 0), jnp.where(has_behind(d), lanes, 0), send, 0)
            return 0
        lax.fori_loop(0, NEAR + 1, step, 0)
        landed[kind, 0, t] = ready[kind, 0, pl.ds(pl.multiple_of(t * piece, piece), piece), :]

    give_back(1, probs, gs)

    gather(1, value)

    for i, cut in enumerate(chunks()):
        o = dot(v_t[...], probs[:, cut]).astype(BF16)
        o_acc[:, cut] = o
        delta[:, cut] = jnp.sum(o.astype(F32) * g_t[:, cut].astype(F32), axis=0, keepdims=True)

    def soft_back(o, _):
        for cut in chunks():
            p = expo[rows_of(o), cut] * factor(o, cut)
            dscores[rows_of(o), cut] = (p * (dprobs[rows_of(o), cut] - delta[:, cut])).astype(BF16)
        return 0
    lax.fori_loop(0, SLOTS, soft_back, 0)

    give_back(0, dscores, qs)

    for n in range(HEADS):
        l, g = n // GROUP, n % GROUP
        part = pl.ds(n * ROWS, ROWS)
        o_out[l, :, pl.ds(g * DIM, DIM)] = o_acc[:, part].T
    for i, cut in enumerate(chunks()):
        dq = (dot(k_t[...], dscores[:, cut]) * SCALE).astype(BF16)
        for j in range(CHUNK // ROWS):
            n = i * (CHUNK // ROWS) + j
            l, g = n // GROUP, n % GROUP
            dq_out[l, :, pl.ds(g * DIM, DIM)] = dq[:, j * ROWS:(j + 1) * ROWS].T

    def back_whole(kind, d, count):
        return pltpu.make_async_remote_copy(
            landed.at[0, 0, pl.ds(0, count)], landed.at[0, 0, pl.ds(0, count)],
            back_send.at[kind, d], back_recv.at[kind, d],
            device_id=partner, device_id_type=MESH,
        )
    for kind in (1, 0):
        for d in range(NEAR + 1):
            @pl.when(has_ahead(d))
            def _(kind=kind, d=d):
                back_whole(kind, d, lanes - (d == 0)).wait_recv()
        for i in range(lanes):
            acc = landed[kind, 0, i].astype(F32)
            for d in range(1, NEAR + 1):
                acc = acc + landed[kind, d, i].astype(F32)
            dkv_ref[kind, :, pl.ds(i * DIM, DIM)] = acc.astype(BF16)

    for kind in range(2):
        for d in range(NEAR + 1):
            @pl.when(has_ahead(d) if d != 3 else has_ahead(1) & has_behind(2))
            def _(kind=kind, d=d):
                whole(keys, kind, d, ROWS - (piece if d == 0 else 0)).wait_send()
            @pl.when(has_behind(d))
            def _(kind=kind, d=d):
                back_whole(kind, d, lanes - (d == 0)).wait_send()
        for e in range(NEAR):
            relayed(kind, e).wait_send()
            swap(kind, e).wait_send()


def store(*refs):
    parts, outs, held, sems = refs[:3], refs[3:6], refs[6:9], refs[9]
    into = [pltpu.make_async_copy(parts[i], held[i], sems.at[i]) for i in range(3)]
    out = [pltpu.make_async_copy(held[i], outs[i], sems.at[3 + i]) for i in range(3)]
    for copy in into:
        copy.start()
    for i in range(3):
        into[i].wait()
        out[i].start()
    for copy in out:
        copy.wait()


def on_device(blocks, lanes, queries, kv_cache, grad_out, positions):
    piece = kv_cache.shape[1]
    wide = kv_cache.shape[2]
    sem = pltpu.SemaphoreType.DMA
    hbm_spec = pl.BlockSpec(memory_space=pltpu.HBM)
    vmem_spec = pl.BlockSpec(memory_space=pltpu.VMEM)
    parts = pl.pallas_call(
        functools.partial(kernel, blocks, lanes),
        out_shape=(
            jax.ShapeDtypeStruct(queries.shape, BF16),
            jax.ShapeDtypeStruct(queries.shape, BF16),
            jax.ShapeDtypeStruct(kv_cache.shape, BF16),
        ),
        in_specs=[hbm_spec] * 4,
        out_specs=(vmem_spec,) * 3,
        scratch_shapes=[
            pltpu.VMEM((2, piece, wide), BF16),
            pltpu.VMEM((1, ROWS), jnp.int32),
            pltpu.VMEM((COLS, DIM), BF16),
            pltpu.VMEM((COLS, DIM), BF16),
            pltpu.VMEM((DIM, COLS), BF16),
            pltpu.VMEM((DIM, COLS), BF16),
            pltpu.VMEM((SLOTS, ROWS, DIM), BF16),
            pltpu.VMEM((SLOTS, ROWS, DIM), BF16),
            pltpu.VMEM((DIM, SLOTS * ROWS), BF16),
            pltpu.VMEM((DIM, SLOTS * ROWS), BF16),
            pltpu.VMEM((SLOTS, ROWS, ROWS), F32),
            pltpu.VMEM((1, COLS), F32),
            pltpu.VMEM((1, COLS), F32),
            pltpu.VMEM((SLOTS, 1, COLS), F32),
            pltpu.VMEM((SLOTS * ROWS, COLS), F32),
            pltpu.VMEM((SLOTS * ROWS, COLS), BF16),
            pltpu.VMEM((SLOTS * ROWS, COLS), F32),
            pltpu.VMEM((SLOTS * ROWS, COLS), BF16),
            pltpu.VMEM((1, COLS), F32),
            pltpu.VMEM((DIM, COLS), BF16),
            pltpu.VMEM((2, NEAR + 1, ROWS, DIM), F32),
            pltpu.VMEM((2, NEAR, ROWS, DIM), F32),
            pltpu.VMEM((2, NEAR, ROWS, DIM), F32),
            pltpu.VMEM((2, NEAR + 1, ROWS, DIM), BF16),
            pltpu.VMEM((2, NEAR + 1, lanes, piece, DIM), BF16),
            sem((4 + 2 * HEADS,)),
            sem((2, NEAR + 1)),
            sem((2, NEAR + 1)),
            sem((2, NEAR)),
            sem((2, NEAR)),
            sem((2, NEAR + 1)),
            sem((2, NEAR + 1)),
            sem((2, NEAR)),
            sem((2, NEAR)),
        ],
        compiler_params=pltpu.CompilerParams(
            collective_id=0, has_side_effects=True, vmem_limit_bytes=61900 * 1024
        ),
    )(queries, kv_cache, grad_out, positions.reshape(1, ROWS))
    return pl.pallas_call(
        store,
        out_shape=tuple(jax.ShapeDtypeStruct(part.shape, part.dtype) for part in parts),
        in_specs=[hbm_spec] * 3,
        out_specs=(hbm_spec,) * 3,
        scratch_shapes=[pltpu.VMEM(part.shape, part.dtype) for part in parts] + [sem((6,))],
        compiler_params=pltpu.CompilerParams(vmem_limit_bytes=61900 * 1024),
    )(*parts)


def solution(mesh):
    return jax.shard_map(
        functools.partial(on_device, mesh.shape["ctx"], mesh.shape["tsp"]),
        mesh=mesh,
        in_specs=(
            P(None, "ctx", "tsp"),
            P(None, ("ctx", "tsp"), None),
            P(None, "ctx", "tsp"),
            P("ctx"),
        ),
        out_specs=(P(None, "ctx", "tsp"), P(None, "ctx", "tsp"), P(None, ("ctx", "tsp"), None)),
        check_vma=False,
    )
```

```python
import functools
import math

import jax
import jax.numpy as jnp
from jax import lax
from jax.experimental import pallas as pl
from jax.experimental.pallas import tpu as pltpu
from jax.sharding import PartitionSpec as P

LAYERS = 2
GROUP = 4
DIM = 128
ROWS = 128
SPAN = 8
NEAR = SPAN // 2
SLOTS = SPAN + 1
HEADS = LAYERS * GROUP
DIRECT = (2, 1, 0)
COLS = HEADS * ROWS
CHUNK = 256
SCALE = DIM ** (-0.5)
TO_EXP2 = SCALE * math.log2(math.e)
LOW = -1e30
MESH = pl.DeviceIdType.MESH
F32 = jnp.float32
BF16 = jnp.bfloat16


def dot(a, b):
    return lax.dot_general(a, b, (((1,), (0,)), ((), ())), preferred_element_type=F32)


def kernel(
    blocks, lanes,
    q_hbm, kv_hbm, g_hbm, pos_hbm,
    o_out, dq_out, dkv_ref,
    kv, pos_ref, qs, gs, q_t, g_t, keys, vals, k_t, v_t, bias,
    top, total, tops, expo, probs, dprobs, dscores, delta, o_acc,
    mine, pair_out, pair_in, ready, landed,
    in_sem, kv_send, kv_recv, pair_send, pair_recv,
    back_send, back_recv, swap_send, swap_recv,
):
    c = lax.axis_index("ctx")
    t = lax.axis_index("tsp")
    core = lax.rem(c, 2)
    partner = (c + 1 - 2 * core, t)
    piece = ROWS // lanes

    def lane(i):
        return lax.rem(t + i, lanes)

    chip = c // 2

    def ahead(d):
        return lax.rem(c + 2 * d, blocks)

    def behind(d):
        return lax.rem(c + blocks - 2 * d, blocks)

    def has_ahead(d):
        return chip + d < blocks // 2

    def has_behind(d):
        return chip >= d

    barrier = pltpu.get_barrier_semaphore()
    pl.semaphore_signal(barrier, inc=1, device_id=partner, device_id_type=MESH)
    for d in DIRECT:
        def hello(i, _, d=d):
            pl.semaphore_signal(barrier, inc=1, device_id=(behind(d), lane(i)), device_id_type=MESH)
            return 0
        @pl.when(has_behind(d))
        def _(d=d, hello=hello):
            lax.fori_loop(1 if d == 0 else 0, lanes, hello, 0)

    kv_copy = pltpu.make_async_copy(kv_hbm, kv, in_sem.at[0])
    kv_copy.start()
    pos_copy = pltpu.make_async_copy(pos_hbm, pos_ref, in_sem.at[3 + 2 * HEADS])
    pos_copy.start()
    def loads():
        out = []
        for l in range(LAYERS):
            for g in range(GROUP):
                n = l * GROUP + g
                cut = pl.ds(g * DIM, DIM)
                out.append(pltpu.make_async_copy(q_hbm.at[l, :, cut], qs.at[pl.ds(n * ROWS, ROWS)], in_sem.at[1 + n]))
                out.append(pltpu.make_async_copy(g_hbm.at[l, :, cut], gs.at[pl.ds(n * ROWS, ROWS)], in_sem.at[1 + HEADS + n]))
        return out
    kv_copy.wait()
    pl.semaphore_wait(barrier, lanes * (1 + sum(jnp.where(has_ahead(d), 1, 0) for d in DIRECT[:-1])))

    def kv_piece(kind, d, i):
        to = lane(i)
        place = (keys if kind == 0 else vals)
        return pltpu.make_async_remote_copy(
            kv.at[kind, :, pl.ds(pl.multiple_of(to * DIM, DIM), DIM)],
            place.at[d, pl.ds(pl.multiple_of(t * piece, piece), piece)],
            kv_send.at[kind, d],
            kv_recv.at[kind, d],
            device_id=(ahead(d), to),
            device_id_type=MESH,
        )
    def own_piece(kind):
        place = (keys if kind == 0 else vals)
        return pltpu.make_async_copy(
            kv.at[kind, :, pl.ds(pl.multiple_of(t * DIM, DIM), DIM)],
            place.at[0, pl.ds(pl.multiple_of(t * piece, piece), piece)],
            in_sem.at[1 + 2 * HEADS + kind],
        )
    for kind in range(2):
        own_piece(kind).start()
        for d in DIRECT:
            def send(i, _, kind=kind, d=d):
                kv_piece(kind, d, i).start()
                return 0
            @pl.when(has_ahead(d))
            def _(d=d, send=send):
                lax.fori_loop(1 if d == 0 else 0, lanes, send, 0)

    for copy in loads():
        copy.start()

    def whole(buf, kind, d, rows=ROWS):
        return pltpu.make_async_remote_copy(
            buf.at[0, pl.ds(0, rows)], buf.at[0, pl.ds(0, rows)],
            kv_send.at[kind, d], kv_recv.at[kind, d],
            device_id=partner, device_id_type=MESH,
        )
    def relay(kind, d):
        place = (keys if kind == 0 else vals)
        e = d - core
        return pltpu.make_async_remote_copy(
            place.at[d], place.at[NEAR + 1 + e],
            pair_send.at[kind, e], pair_recv.at[kind, e],
            device_id=partner, device_id_type=MESH,
        )
    def relayed(kind, e):
        place = (keys if kind == 0 else vals)
        return pltpu.make_async_remote_copy(
            place.at[e + core], place.at[NEAR + 1 + e],
            pair_send.at[kind, e], pair_recv.at[kind, e],
            device_id=partner, device_id_type=MESH,
        )

    for d in range(1, NEAR + 1):
        @pl.when(jnp.logical_not(has_behind(d)))
        def _(d=d):
            keys[d] = jnp.zeros((ROWS, DIM), BF16)
            vals[d] = jnp.zeros((ROWS, DIM), BF16)
        @pl.when(jnp.logical_not(has_ahead(d)))
        def _(d=d):
            for kind in range(2):
                landed[kind, d] = jnp.zeros(landed.shape[2:], BF16)

    for copy in loads():
        copy.wait()
    for n in range(HEADS):
        part = pl.ds(n * ROWS, ROWS)
        q_t[:, part] = qs[part].T
        g_t[:, part] = gs[part].T
    pos_copy.wait()
    pos = pos_ref[...]
    base = lax.broadcasted_iota(jnp.int32, (ROWS, ROWS), 1) - lax.broadcasted_iota(jnp.int32, (ROWS, ROWS), 0)
    def mask(o, _):
        blocks_back = jnp.where(o <= NEAR, 2 * o, 2 * (o - NEAR) - 1)
        distance = base + blocks_back * ROWS
        visible = (distance >= 0) & (distance <= pos) & (distance < SPAN * ROWS)
        bias[o] = jnp.where(visible, 0.0, -jnp.inf)
        return 0
    lax.fori_loop(0, SLOTS, mask, 0)
    top[...] = jnp.full(top.shape, LOW, F32)
    total[...] = jnp.zeros(total.shape, F32)

    def chunks():
        return [pl.ds(i * CHUNK, CHUNK) for i in range(COLS // CHUNK)]

    def rows_of(o):
        if isinstance(o, int):
            return pl.ds(o * ROWS, ROWS)
        return pl.ds(pl.multiple_of(o * ROWS, ROWS), ROWS)

    def score(o):
        block = keys[o]
        hide = jnp.concatenate([bias[o]] * (CHUNK // ROWS), axis=1)
        for cut in chunks():
            s = dot(block, q_t[:, cut]) + hide
            before = top[:, cut]
            now = jnp.maximum(before, jnp.max(s, axis=0, keepdims=True))
            e = jnp.exp2((s - now) * TO_EXP2)
            total[:, cut] = total[:, cut] * jnp.exp2((before - now) * TO_EXP2) + jnp.sum(e, axis=0, keepdims=True)
            top[:, cut] = now
            tops[o, :, cut] = now
            expo[rows_of(o), cut] = e
        k_t[:, rows_of(o)] = block.T

    def value(o):
        block = vals[o]
        for cut in chunks():
            dprobs[rows_of(o), cut] = dot(block, g_t[:, cut])
        v_t[:, rows_of(o)] = block.T

    def forward(kind, hop):
        place = (keys if kind == 0 else vals)
        return pltpu.make_async_remote_copy(
            place.at[2], place.at[2 + hop],
            kv_send.at[kind, 2 + hop], kv_recv.at[kind, 2 + hop],
            device_id=(ahead(hop), t), device_id_type=MESH,
        )
    def first(kind):
        @pl.when(has_behind(2))
        def _():
            whole((keys if kind == 0 else vals), kind, 2).wait_recv()
            for hop in (2, 1):
                @pl.when(has_ahead(hop))
                def _(hop=hop):
                    forward(kind, hop).start()
        relay(kind, 2).start()

    def gather(kind, use, between=None):
        place = (keys if kind == 0 else vals)
        def pair(d):
            e = d - 1 + core
            @pl.when((e >= 0) & (e < NEAR))
            def _():
                relayed(kind, e).wait_recv()
                use(NEAR + 1 + e)
        def order(i):
            return jnp.where(i == 0, 2, jnp.where(i < 3, i - 1, 7 - i))
        use(2)
        def step(i, _):
            d = order(i)
            @pl.when(d == 0)
            def _():
                own_piece(kind).wait()
                whole(place, kind, 0, ROWS - piece).wait_recv()
            @pl.when((d > 0) & has_behind(d))
            def _():
                whole(place, kind, d).wait_recv()
            @pl.when((d - core >= 0) & (d - core < NEAR))
            def _():
                relay(kind, d).start()
            use(d)
            pair(order(i - 1))
            return 0
        lax.fori_loop(1, NEAR + 1, step, 0)
        if between is not None:
            between()
        pair(3)

    first(0)
    gather(0, score, lambda: first(1))

    def factor(o, cut):
        return tops[o, :, cut]

    inverse = 1.0 / total[...]
    last = top[...]
    def scales(o, _):
        tops[o] = jnp.exp2((tops[o] - last) * TO_EXP2) * inverse
        return 0
    lax.fori_loop(0, SLOTS, scales, 0)
    def soft(o, _):
        for cut in chunks():
            probs[rows_of(o), cut] = (expo[rows_of(o), cut] * factor(o, cut)).astype(BF16)
        return 0

    def swap(kind, e):
        return pltpu.make_async_remote_copy(
            pair_out.at[kind, e], pair_in.at[kind, e],
            swap_send.at[kind, e], swap_recv.at[kind, e],
            device_id=partner, device_id_type=MESH,
        )
    def back_piece(kind, d, i):
        to = lane(i)
        return pltpu.make_async_remote_copy(
            ready.at[kind, d, pl.ds(pl.multiple_of(to * piece, piece), piece)],
            landed.at[kind, d, t],
            back_send.at[kind, d],
            back_recv.at[kind, d],
            device_id=(behind(d), to),
            device_id_type=MESH,
        )
    def give_back(kind, prepare, left, right):
        lax.fori_loop(NEAR + 1, SLOTS, prepare, 0)
        odd = dot(left[pl.ds((NEAR + 1) * ROWS, NEAR * ROWS), :], right[...])
        for e in range(NEAR):
            pair_out[kind, e] = odd[e * ROWS:(e + 1) * ROWS].astype(BF16)
            swap(kind, e).start()
        lax.fori_loop(0, NEAR + 1, prepare, 0)
        even = dot(left[pl.ds(0, (NEAR + 1) * ROWS), :], right[...])
        for d in range(NEAR + 1):
            mine[kind, d] = even[d * ROWS:(d + 1) * ROWS]
        def step(i, _):
            d = NEAR - i
            e = d - core
            paired = (e >= 0) & (e < NEAR)
            @pl.when(paired)
            def _():
                swap(kind, e).wait_recv()
                both = mine[kind, d] + pair_in[kind, e].astype(F32)
                ready[kind, d] = (both if kind == 1 else both * SCALE).astype(BF16)
            @pl.when(jnp.logical_not(paired))
            def _():
                ready[kind, d] = (mine[kind, d] if kind == 1 else mine[kind, d] * SCALE).astype(BF16)
            def send(i, _):
                back_piece(kind, d, i).start()
                return 0
            lax.fori_loop(jnp.where(d == 0, 1, 0), jnp.where(has_behind(d), lanes, 0), send, 0)
            return 0
        lax.fori_loop(0, NEAR + 1, step, 0)
        landed[kind, 0, t] = ready[kind, 0, pl.ds(pl.multiple_of(t * piece, piece), piece), :]

    give_back(1, soft, probs, gs)

    gather(1, value)

    for i, cut in enumerate(chunks()):
        o = dot(v_t[...], probs[:, cut]).astype(BF16)
        o_acc[:, cut] = o
        delta[:, cut] = jnp.sum(o.astype(F32) * g_t[:, cut].astype(F32), axis=0, keepdims=True)

    def soft_back(o, _):
        for cut in chunks():
            p = expo[rows_of(o), cut] * factor(o, cut)
            dscores[rows_of(o), cut] = (p * (dprobs[rows_of(o), cut] - delta[:, cut])).astype(BF16)
        return 0

    give_back(0, soft_back, dscores, qs)

    for n in range(HEADS):
        l, g = n // GROUP, n % GROUP
        part = pl.ds(n * ROWS, ROWS)
        o_out[l, :, pl.ds(g * DIM, DIM)] = o_acc[:, part].T
    for i, cut in enumerate(chunks()):
        dq = (dot(k_t[...], dscores[:, cut]) * SCALE).astype(BF16)
        for j in range(CHUNK // ROWS):
            n = i * (CHUNK // ROWS) + j
            l, g = n // GROUP, n % GROUP
            dq_out[l, :, pl.ds(g * DIM, DIM)] = dq[:, j * ROWS:(j + 1) * ROWS].T

    def back_whole(kind, d, count):
        return pltpu.make_async_remote_copy(
            landed.at[0, 0, pl.ds(0, count)], landed.at[0, 0, pl.ds(0, count)],
            back_send.at[kind, d], back_recv.at[kind, d],
            device_id=partner, device_id_type=MESH,
        )
    for kind in (1, 0):
        for d in range(NEAR + 1):
            @pl.when(has_ahead(d))
            def _(kind=kind, d=d):
                back_whole(kind, d, lanes - (d == 0)).wait_recv()
        for i in range(lanes):
            acc = landed[kind, 0, i].astype(F32)
            for d in range(1, NEAR + 1):
                acc = acc + landed[kind, d, i].astype(F32)
            dkv_ref[kind, :, pl.ds(i * DIM, DIM)] = acc.astype(BF16)

    for kind in range(2):
        for d in range(NEAR + 1):
            @pl.when(has_ahead(d) if d < 3 else has_ahead(d - 2) & has_behind(2))
            def _(kind=kind, d=d):
                whole(keys, kind, d, ROWS - (piece if d == 0 else 0)).wait_send()
            @pl.when(has_behind(d))
            def _(kind=kind, d=d):
                back_whole(kind, d, lanes - (d == 0)).wait_send()
        for e in range(NEAR):
            relayed(kind, e).wait_send()
            swap(kind, e).wait_send()


def store(*refs):
    parts, outs, held, sems = refs[:3], refs[3:6], refs[6:9], refs[9]
    into = [pltpu.make_async_copy(parts[i], held[i], sems.at[i]) for i in range(3)]
    out = [pltpu.make_async_copy(held[i], outs[i], sems.at[3 + i]) for i in range(3)]
    for copy in into:
        copy.start()
    for i in range(3):
        into[i].wait()
        out[i].start()
    for copy in out:
        copy.wait()


def on_device(blocks, lanes, queries, kv_cache, grad_out, positions):
    piece = kv_cache.shape[1]
    wide = kv_cache.shape[2]
    sem = pltpu.SemaphoreType.DMA
    hbm_spec = pl.BlockSpec(memory_space=pltpu.HBM)
    vmem_spec = pl.BlockSpec(memory_space=pltpu.VMEM)
    parts = pl.pallas_call(
        functools.partial(kernel, blocks, lanes),
        out_shape=(
            jax.ShapeDtypeStruct(queries.shape, BF16),
            jax.ShapeDtypeStruct(queries.shape, BF16),
            jax.ShapeDtypeStruct(kv_cache.shape, BF16),
        ),
        in_specs=[hbm_spec] * 4,
        out_specs=(vmem_spec,) * 3,
        scratch_shapes=[
            pltpu.VMEM((2, piece, wide), BF16),
            pltpu.VMEM((1, ROWS), jnp.int32),
            pltpu.VMEM((COLS, DIM), BF16),
            pltpu.VMEM((COLS, DIM), BF16),
            pltpu.VMEM((DIM, COLS), BF16),
            pltpu.VMEM((DIM, COLS), BF16),
            pltpu.VMEM((SLOTS, ROWS, DIM), BF16),
            pltpu.VMEM((SLOTS, ROWS, DIM), BF16),
            pltpu.VMEM((DIM, SLOTS * ROWS), BF16),
            pltpu.VMEM((DIM, SLOTS * ROWS), BF16),
            pltpu.VMEM((SLOTS, ROWS, ROWS), F32),
            pltpu.VMEM((1, COLS), F32),
            pltpu.VMEM((1, COLS), F32),
            pltpu.VMEM((SLOTS, 1, COLS), F32),
            pltpu.VMEM((SLOTS * ROWS, COLS), F32),
            pltpu.VMEM((SLOTS * ROWS, COLS), BF16),
            pltpu.VMEM((SLOTS * ROWS, COLS), F32),
            pltpu.VMEM((SLOTS * ROWS, COLS), BF16),
            pltpu.VMEM((1, COLS), F32),
            pltpu.VMEM((DIM, COLS), BF16),
            pltpu.VMEM((2, NEAR + 1, ROWS, DIM), F32),
            pltpu.VMEM((2, NEAR, ROWS, DIM), BF16),
            pltpu.VMEM((2, NEAR, ROWS, DIM), BF16),
            pltpu.VMEM((2, NEAR + 1, ROWS, DIM), BF16),
            pltpu.VMEM((2, NEAR + 1, lanes, piece, DIM), BF16),
            sem((4 + 2 * HEADS,)),
            sem((2, NEAR + 1)),
            sem((2, NEAR + 1)),
            sem((2, NEAR)),
            sem((2, NEAR)),
            sem((2, NEAR + 1)),
            sem((2, NEAR + 1)),
            sem((2, NEAR)),
            sem((2, NEAR)),
        ],
        compiler_params=pltpu.CompilerParams(
            collective_id=0, has_side_effects=True, vmem_limit_bytes=61900 * 1024
        ),
    )(queries, kv_cache, grad_out, positions.reshape(1, ROWS))
    return pl.pallas_call(
        store,
        out_shape=tuple(jax.ShapeDtypeStruct(part.shape, part.dtype) for part in parts),
        in_specs=[hbm_spec] * 3,
        out_specs=(hbm_spec,) * 3,
        scratch_shapes=[pltpu.VMEM(part.shape, part.dtype) for part in parts] + [sem((6,))],
        compiler_params=pltpu.CompilerParams(vmem_limit_bytes=61900 * 1024),
    )(*parts)


def solution(mesh):
    return jax.shard_map(
        functools.partial(on_device, mesh.shape["ctx"], mesh.shape["tsp"]),
        mesh=mesh,
        in_specs=(
            P(None, "ctx", "tsp"),
            P(None, ("ctx", "tsp"), None),
            P(None, "ctx", "tsp"),
            P("ctx"),
        ),
        out_specs=(P(None, "ctx", "tsp"), P(None, "ctx", "tsp"), P(None, ("ctx", "tsp"), None)),
        check_vma=False,
    )
```

```python
import functools
import math

import jax
import jax.numpy as jnp
from jax import lax
from jax.experimental import pallas as pl
from jax.experimental.pallas import tpu as pltpu
from jax.sharding import PartitionSpec as P

LAYERS = 2
GROUP = 4
DIM = 128
ROWS = 128
SPAN = 8
NEAR = SPAN // 2
SLOTS = SPAN + 1
HEADS = LAYERS * GROUP
DIRECT = (2, 1, 0)
COLS = HEADS * ROWS
CHUNK = 256
SCALE = DIM ** (-0.5)
TO_EXP2 = SCALE * math.log2(math.e)
LOW = -1e30
MESH = pl.DeviceIdType.MESH
F32 = jnp.float32
BF16 = jnp.bfloat16


def dot(a, b):
    return lax.dot_general(a, b, (((1,), (0,)), ((), ())), preferred_element_type=F32)


def kernel(
    blocks, lanes,
    q_hbm, kv_hbm, g_hbm, pos_hbm,
    o_hbm, dq_hbm, dkv_ref,
    kv, pos_ref, qs, gs, q_t, g_t, keys, vals, k_t, v_t, bias,
    top, total, tops, expo, probs, dprobs, dscores, delta, o_acc,
    mine, pair_out, pair_in, ready, landed, o_out, dq_out,
    in_sem, out_sem, kv_send, kv_recv, pair_send, pair_recv,
    back_send, back_recv, swap_send, swap_recv,
):
    c = lax.axis_index("ctx")
    t = lax.axis_index("tsp")
    core = lax.rem(c, 2)
    partner = (c + 1 - 2 * core, t)
    piece = ROWS // lanes

    def lane(i):
        return lax.rem(t + i, lanes)

    chip = c // 2

    def ahead(d):
        return lax.rem(c + 2 * d, blocks)

    def behind(d):
        return lax.rem(c + blocks - 2 * d, blocks)

    def has_ahead(d):
        return chip + d < blocks // 2

    def has_behind(d):
        return chip >= d

    barrier = pltpu.get_barrier_semaphore()
    pl.semaphore_signal(barrier, inc=1, device_id=partner, device_id_type=MESH)
    for d in DIRECT:
        def hello(i, _, d=d):
            pl.semaphore_signal(barrier, inc=1, device_id=(behind(d), lane(i)), device_id_type=MESH)
            return 0
        @pl.when(has_behind(d))
        def _(d=d, hello=hello):
            lax.fori_loop(1 if d == 0 else 0, lanes, hello, 0)

    kv_copy = pltpu.make_async_copy(kv_hbm, kv, in_sem.at[0])
    kv_copy.start()
    pos_copy = pltpu.make_async_copy(pos_hbm, pos_ref, in_sem.at[3 + 2 * HEADS])
    pos_copy.start()
    def loads():
        out = []
        for l in range(LAYERS):
            for g in range(GROUP):
                n = l * GROUP + g
                cut = pl.ds(g * DIM, DIM)
                out.append(pltpu.make_async_copy(q_hbm.at[l, :, cut], qs.at[pl.ds(n * ROWS, ROWS)], in_sem.at[1 + n]))
                out.append(pltpu.make_async_copy(g_hbm.at[l, :, cut], gs.at[pl.ds(n * ROWS, ROWS)], in_sem.at[1 + HEADS + n]))
        return out
    kv_copy.wait()
    pl.semaphore_wait(barrier, lanes * (1 + sum(jnp.where(has_ahead(d), 1, 0) for d in DIRECT[:-1])))

    def kv_piece(kind, d, i):
        to = lane(i)
        place = (keys if kind == 0 else vals)
        return pltpu.make_async_remote_copy(
            kv.at[kind, :, pl.ds(pl.multiple_of(to * DIM, DIM), DIM)],
            place.at[d, pl.ds(pl.multiple_of(t * piece, piece), piece)],
            kv_send.at[kind, d],
            kv_recv.at[kind, d],
            device_id=(ahead(d), to),
            device_id_type=MESH,
        )
    def own_piece(kind):
        place = (keys if kind == 0 else vals)
        return pltpu.make_async_copy(
            kv.at[kind, :, pl.ds(pl.multiple_of(t * DIM, DIM), DIM)],
            place.at[0, pl.ds(pl.multiple_of(t * piece, piece), piece)],
            in_sem.at[1 + 2 * HEADS + kind],
        )
    for kind in range(2):
        own_piece(kind).start()
        for d in DIRECT:
            def send(i, _, kind=kind, d=d):
                kv_piece(kind, d, i).start()
                return 0
            @pl.when(has_ahead(d))
            def _(d=d, send=send):
                lax.fori_loop(1 if d == 0 else 0, lanes, send, 0)

    for copy in loads():
        copy.start()

    def whole(buf, kind, d, rows=ROWS):
        return pltpu.make_async_remote_copy(
            buf.at[0, pl.ds(0, rows)], buf.at[0, pl.ds(0, rows)],
            kv_send.at[kind, d], kv_recv.at[kind, d],
            device_id=partner, device_id_type=MESH,
        )
    def relay(kind, d):
        place = (keys if kind == 0 else vals)
        e = d - core
        return pltpu.make_async_remote_copy(
            place.at[d], place.at[NEAR + 1 + e],
            pair_send.at[kind, e], pair_recv.at[kind, e],
            device_id=partner, device_id_type=MESH,
        )
    def relayed(kind, e):
        place = (keys if kind == 0 else vals)
        return pltpu.make_async_remote_copy(
            place.at[e + core], place.at[NEAR + 1 + e],
            pair_send.at[kind, e], pair_recv.at[kind, e],
            device_id=partner, device_id_type=MESH,
        )

    for d in range(1, NEAR + 1):
        @pl.when(jnp.logical_not(has_behind(d)))
        def _(d=d):
            keys[d] = jnp.zeros((ROWS, DIM), BF16)
            vals[d] = jnp.zeros((ROWS, DIM), BF16)
        @pl.when(jnp.logical_not(has_ahead(d)))
        def _(d=d):
            for kind in range(2):
                landed[kind, d] = jnp.zeros(landed.shape[2:], BF16)

    for copy in loads():
        copy.wait()
    for n in range(HEADS):
        part = pl.ds(n * ROWS, ROWS)
        q_t[:, part] = qs[part].T
        g_t[:, part] = gs[part].T
    pos_copy.wait()
    pos = pos_ref[...]
    base = lax.broadcasted_iota(jnp.int32, (ROWS, ROWS), 1) - lax.broadcasted_iota(jnp.int32, (ROWS, ROWS), 0)
    def mask(o, _):
        blocks_back = jnp.where(o <= NEAR, 2 * o, 2 * (o - NEAR) - 1)
        distance = base + blocks_back * ROWS
        visible = (distance >= 0) & (distance <= pos) & (distance < SPAN * ROWS)
        bias[o] = jnp.where(visible, 0.0, -jnp.inf)
        return 0
    lax.fori_loop(0, SLOTS, mask, 0)
    top[...] = jnp.full(top.shape, LOW, F32)
    total[...] = jnp.zeros(total.shape, F32)

    def chunks():
        return [pl.ds(i * CHUNK, CHUNK) for i in range(COLS // CHUNK)]

    def rows_of(o):
        if isinstance(o, int):
            return pl.ds(o * ROWS, ROWS)
        return pl.ds(pl.multiple_of(o * ROWS, ROWS), ROWS)

    def score(o):
        block = keys[o]
        hide = jnp.concatenate([bias[o]] * (CHUNK // ROWS), axis=1)
        for cut in chunks():
            s = dot(block, q_t[:, cut]) + hide
            before = top[:, cut]
            now = jnp.maximum(before, jnp.max(s, axis=0, keepdims=True))
            e = jnp.exp2((s - now) * TO_EXP2)
            total[:, cut] = total[:, cut] * jnp.exp2((before - now) * TO_EXP2) + jnp.sum(e, axis=0, keepdims=True)
            top[:, cut] = now
            tops[o, :, cut] = now
            expo[rows_of(o), cut] = e
        k_t[:, rows_of(o)] = block.T

    def value(o):
        block = vals[o]
        for cut in chunks():
            dprobs[rows_of(o), cut] = dot(block, g_t[:, cut])
        v_t[:, rows_of(o)] = block.T

    def forward(kind, hop):
        place = (keys if kind == 0 else vals)
        return pltpu.make_async_remote_copy(
            place.at[2], place.at[2 + hop],
            kv_send.at[kind, 2 + hop], kv_recv.at[kind, 2 + hop],
            device_id=(ahead(hop), t), device_id_type=MESH,
        )
    def first(kind):
        @pl.when(has_behind(2))
        def _():
            whole((keys if kind == 0 else vals), kind, 2).wait_recv()
            for hop in (2, 1):
                @pl.when(has_ahead(hop))
                def _(hop=hop):
                    forward(kind, hop).start()
        relay(kind, 2).start()

    def gather(kind, use, between=None):
        place = (keys if kind == 0 else vals)
        def pair(d):
            e = d - 1 + core
            @pl.when((e >= 0) & (e < NEAR))
            def _():
                relayed(kind, e).wait_recv()
                use(NEAR + 1 + e)
        def order(i):
            return jnp.where(i == 0, 2, jnp.where(i < 3, i - 1, 7 - i))
        use(2)
        def step(i, _):
            d = order(i)
            @pl.when(d == 0)
            def _():
                own_piece(kind).wait()
                whole(place, kind, 0, ROWS - piece).wait_recv()
            @pl.when((d > 0) & has_behind(d))
            def _():
                whole(place, kind, d).wait_recv()
            @pl.when((d - core >= 0) & (d - core < NEAR))
            def _():
                relay(kind, d).start()
            use(d)
            pair(order(i - 1))
            return 0
        lax.fori_loop(1, NEAR + 1, step, 0)
        if between is not None:
            between()
        pair(3)

    first(0)
    gather(0, score, lambda: first(1))

    def factor(o, cut):
        return tops[o, :, cut]

    inverse = 1.0 / total[...]
    last = top[...]
    def scales(o, _):
        tops[o] = jnp.exp2((tops[o] - last) * TO_EXP2) * inverse
        return 0
    lax.fori_loop(0, SLOTS, scales, 0)
    def soft(o, _):
        for cut in chunks():
            probs[rows_of(o), cut] = (expo[rows_of(o), cut] * factor(o, cut)).astype(BF16)
        return 0

    def swap(kind, e):
        return pltpu.make_async_remote_copy(
            pair_out.at[kind, e], pair_in.at[kind, e],
            swap_send.at[kind, e], swap_recv.at[kind, e],
            device_id=partner, device_id_type=MESH,
        )
    def back_piece(kind, d, i):
        to = lane(i)
        return pltpu.make_async_remote_copy(
            ready.at[kind, d, pl.ds(pl.multiple_of(to * piece, piece), piece)],
            landed.at[kind, d, t],
            back_send.at[kind, d],
            back_recv.at[kind, d],
            device_id=(behind(d), to),
            device_id_type=MESH,
        )
    def give_back(kind, prepare, left, right):
        lax.fori_loop(NEAR + 1, SLOTS, prepare, 0)
        odd = dot(left[pl.ds((NEAR + 1) * ROWS, NEAR * ROWS), :], right[...])
        for e in range(NEAR):
            pair_out[kind, e] = odd[e * ROWS:(e + 1) * ROWS].astype(BF16)
            swap(kind, e).start()
        lax.fori_loop(0, NEAR + 1, prepare, 0)
        even = dot(left[pl.ds(0, (NEAR + 1) * ROWS), :], right[...])
        for d in range(NEAR + 1):
            mine[kind, d] = even[d * ROWS:(d + 1) * ROWS]
        def step(i, _):
            d = NEAR - i
            e = d - core
            paired = (e >= 0) & (e < NEAR)
            @pl.when(paired)
            def _():
                swap(kind, e).wait_recv()
                both = mine[kind, d] + pair_in[kind, e].astype(F32)
                ready[kind, d] = (both if kind == 1 else both * SCALE).astype(BF16)
            @pl.when(jnp.logical_not(paired))
            def _():
                ready[kind, d] = (mine[kind, d] if kind == 1 else mine[kind, d] * SCALE).astype(BF16)
            def send(i, _):
                back_piece(kind, d, i).start()
                return 0
            lax.fori_loop(jnp.where(d == 0, 1, 0), jnp.where(has_behind(d), lanes, 0), send, 0)
            return 0
        lax.fori_loop(0, NEAR + 1, step, 0)
        landed[kind, 0, t] = ready[kind, 0, pl.ds(pl.multiple_of(t * piece, piece), piece), :]

    give_back(1, soft, probs, gs)

    gather(1, value)

    for i, cut in enumerate(chunks()):
        o = dot(v_t[...], probs[:, cut]).astype(BF16)
        o_acc[:, cut] = o
        delta[:, cut] = jnp.sum(o.astype(F32) * g_t[:, cut].astype(F32), axis=0, keepdims=True)

    def soft_back(o, _):
        for cut in chunks():
            p = expo[rows_of(o), cut] * factor(o, cut)
            dscores[rows_of(o), cut] = (p * (dprobs[rows_of(o), cut] - delta[:, cut])).astype(BF16)
        return 0

    give_back(0, soft_back, dscores, qs)

    for n in range(HEADS):
        l, g = n // GROUP, n % GROUP
        part = pl.ds(n * ROWS, ROWS)
        o_out[l, :, pl.ds(g * DIM, DIM)] = o_acc[:, part].T
    o_copy = pltpu.make_async_copy(o_out, o_hbm, out_sem.at[0])
    o_copy.start()
    for i, cut in enumerate(chunks()):
        dq = (dot(k_t[...], dscores[:, cut]) * SCALE).astype(BF16)
        for j in range(CHUNK // ROWS):
            n = i * (CHUNK // ROWS) + j
            l, g = n // GROUP, n % GROUP
            dq_out[l, :, pl.ds(g * DIM, DIM)] = dq[:, j * ROWS:(j + 1) * ROWS].T

    dq_copy = pltpu.make_async_copy(dq_out, dq_hbm, out_sem.at[1])
    dq_copy.start()

    def back_whole(kind, d, count):
        return pltpu.make_async_remote_copy(
            landed.at[0, 0, pl.ds(0, count)], landed.at[0, 0, pl.ds(0, count)],
            back_send.at[kind, d], back_recv.at[kind, d],
            device_id=partner, device_id_type=MESH,
        )
    for kind in (1, 0):
        if kind == 0:
            o_copy.wait()
            dq_copy.wait()
        for d in range(NEAR + 1):
            @pl.when(has_ahead(d))
            def _(kind=kind, d=d):
                back_whole(kind, d, lanes - (d == 0)).wait_recv()
        for i in range(lanes):
            acc = landed[kind, 0, i].astype(F32)
            for d in range(1, NEAR + 1):
                acc = acc + landed[kind, d, i].astype(F32)
            dkv_ref[kind, :, pl.ds(i * DIM, DIM)] = acc.astype(BF16)

    for kind in range(2):
        for d in range(NEAR + 1):
            @pl.when(has_ahead(d) if d < 3 else has_ahead(d - 2) & has_behind(2))
            def _(kind=kind, d=d):
                whole(keys, kind, d, ROWS - (piece if d == 0 else 0)).wait_send()
            @pl.when(has_behind(d))
            def _(kind=kind, d=d):
                back_whole(kind, d, lanes - (d == 0)).wait_send()
        for e in range(NEAR):
            relayed(kind, e).wait_send()
            swap(kind, e).wait_send()


def store(*refs):
    parts, outs, held, sems = refs[:3], refs[3:6], refs[6:9], refs[9]
    into = [pltpu.make_async_copy(parts[i], held[i], sems.at[i]) for i in range(3)]
    out = [pltpu.make_async_copy(held[i], outs[i], sems.at[3 + i]) for i in range(3)]
    for copy in into:
        copy.start()
    for i in range(3):
        into[i].wait()
        out[i].start()
    for copy in out:
        copy.wait()


def on_device(blocks, lanes, queries, kv_cache, grad_out, positions):
    piece = kv_cache.shape[1]
    wide = kv_cache.shape[2]
    sem = pltpu.SemaphoreType.DMA
    hbm_spec = pl.BlockSpec(memory_space=pltpu.HBM)
    vmem_spec = pl.BlockSpec(memory_space=pltpu.VMEM)
    parts = pl.pallas_call(
        functools.partial(kernel, blocks, lanes),
        out_shape=(
            jax.ShapeDtypeStruct(queries.shape, BF16),
            jax.ShapeDtypeStruct(queries.shape, BF16),
            jax.ShapeDtypeStruct(kv_cache.shape, BF16),
        ),
        in_specs=[hbm_spec] * 4,
        out_specs=(hbm_spec, hbm_spec, vmem_spec),
        scratch_shapes=[
            pltpu.VMEM((2, piece, wide), BF16),
            pltpu.VMEM((1, ROWS), jnp.int32),
            pltpu.VMEM((COLS, DIM), BF16),
            pltpu.VMEM((COLS, DIM), BF16),
            pltpu.VMEM((DIM, COLS), BF16),
            pltpu.VMEM((DIM, COLS), BF16),
            pltpu.VMEM((SLOTS, ROWS, DIM), BF16),
            pltpu.VMEM((SLOTS, ROWS, DIM), BF16),
            pltpu.VMEM((DIM, SLOTS * ROWS), BF16),
            pltpu.VMEM((DIM, SLOTS * ROWS), BF16),
            pltpu.VMEM((SLOTS, ROWS, ROWS), F32),
            pltpu.VMEM((1, COLS), F32),
            pltpu.VMEM((1, COLS), F32),
            pltpu.VMEM((SLOTS, 1, COLS), F32),
            pltpu.VMEM((SLOTS * ROWS, COLS), F32),
            pltpu.VMEM((SLOTS * ROWS, COLS), BF16),
            pltpu.VMEM((SLOTS * ROWS, COLS), F32),
            pltpu.VMEM((SLOTS * ROWS, COLS), BF16),
            pltpu.VMEM((1, COLS), F32),
            pltpu.VMEM((DIM, COLS), BF16),
            pltpu.VMEM((2, NEAR + 1, ROWS, DIM), F32),
            pltpu.VMEM((2, NEAR, ROWS, DIM), BF16),
            pltpu.VMEM((2, NEAR, ROWS, DIM), BF16),
            pltpu.VMEM((2, NEAR + 1, ROWS, DIM), BF16),
            pltpu.VMEM((2, NEAR + 1, lanes, piece, DIM), BF16),
            pltpu.VMEM(queries.shape, BF16),
            pltpu.VMEM(queries.shape, BF16),
            sem((4 + 2 * HEADS,)),
            sem((2,)),
            sem((2, NEAR + 1)),
            sem((2, NEAR + 1)),
            sem((2, NEAR)),
            sem((2, NEAR)),
            sem((2, NEAR + 1)),
            sem((2, NEAR + 1)),
            sem((2, NEAR)),
            sem((2, NEAR)),
        ],
        compiler_params=pltpu.CompilerParams(
            collective_id=0, has_side_effects=True, vmem_limit_bytes=61900 * 1024
        ),
    )(queries, kv_cache, grad_out, positions.reshape(1, ROWS))
    return pl.pallas_call(
        store,
        out_shape=tuple(jax.ShapeDtypeStruct(part.shape, part.dtype) for part in parts),
        in_specs=[hbm_spec] * 3,
        out_specs=(hbm_spec,) * 3,
        scratch_shapes=[pltpu.VMEM(part.shape, part.dtype) for part in parts] + [sem((6,))],
        compiler_params=pltpu.CompilerParams(vmem_limit_bytes=61900 * 1024),
    )(*parts)


def solution(mesh):
    return jax.shard_map(
        functools.partial(on_device, mesh.shape["ctx"], mesh.shape["tsp"]),
        mesh=mesh,
        in_specs=(
            P(None, "ctx", "tsp"),
            P(None, ("ctx", "tsp"), None),
            P(None, "ctx", "tsp"),
            P("ctx"),
        ),
        out_specs=(P(None, "ctx", "tsp"), P(None, "ctx", "tsp"), P(None, ("ctx", "tsp"), None)),
        check_vma=False,
    )
```
